256 devices in a mesh: row: 4 (over x), col: 8 (over y, z_lo), depth: 8 (over z_hi, core).
Axes of the slice: x: 4, y: 4, z: 8 (z_hi: 4, z_lo: 2; z = z_hi * 2 + z_lo), core: 2. Of those that a mesh axis runs over, the one named last changes fastest.
Arguments:
- features: bfloat16 [256, 16384], P('depth', ('row', 'col')), may hold values from -6 to 6
- weight: bfloat16 [256, 256], replicated, may hold values from -0.375 to 0.375
- tiles: bfloat16 [4, 8, 8, 64, 128, 128], P('row', 'col', 'depth'), may hold values from -0.03125 to 0.03125
- pairs: int32 [4, 8, 8, 2, 64], P('row', 'col', 'depth'), may hold values from 0 to 31, as said below
- counts: int32 [4, 8, 8], P('row', 'col', 'depth'), may hold values from 16 to 64, as said below
- cotangent: bfloat16 [256, 16384], P('depth', ('row', 'col')), may hold values from -6 to 6
Outputs:
- activation: bfloat16 [256, 16384], P('depth', ('row', 'col'))
- weight_grad: float32 [256, 256], P(None, 'depth')
The draws below stay inside these ranges and needn't reach their ends.
Inputs may be any that keep to these rules, and one draw needn't show every extreme that they name: `pairs`: each device's local block numbers: row blocks below 32, column blocks below 16. Within one grid cell (r, c), no two slots of its devices along depth name the same pair of blocks. `counts`: slots at and past a device's count hold values that are not part of the adjacency.
All inputs are finite; a program needn't handle non-finite values.
Results may differ from the reference program's by a relative error of at most 0.0051.
Values may be sent and summed in bfloat16 or wider, within the bound.
No kernel may reach another device: no remote copies, remote signals or barrier semaphores. Data moves between devices by JAX's collectives and lax.ppermute only.
A program may use at most 64 MiB of HBM per device.

```python
import jax
import jax.numpy as jnp
from jax import lax

FEAT = 256
TILE = 128
NODE_DEV = 512
TILES_DEV = 64
NODES = 16384
N_ROW = 4
N_COL = 8
N_DEPTH = 8


def draw_counts(key, part):
    key = jax.random.fold_in(key, 11)
    devices_all = N_ROW * N_COL * N_DEPTH
    first_key, second_key, third_key = jax.random.split(key, 3)
    lowest = max(1, TILES_DEV // 4)
    base_counts = jax.random.randint(first_key, (devices_all,), lowest, TILES_DEV // 2 + 1)
    heavy_cells = jax.random.randint(second_key, (devices_all,), 0, 8) == 0
    chosen_cell = jax.random.randint(third_key, (), 0, devices_all)
    positions = jnp.arange(devices_all)
    result = jnp.where(heavy_cells | (positions == chosen_cell), TILES_DEV, base_counts)
    return result.reshape(N_ROW, N_COL, N_DEPTH).astype(jnp.int32)


def draw_pairs(key, part):
    key = jax.random.fold_in(key, 23)
    cells_all = N_ROW * N_COL
    row_blocks = N_COL * NODE_DEV // TILE
    col_blocks = N_ROW * NODE_DEV // TILE
    position_total = row_blocks * col_blocks
    taken = N_DEPTH * TILES_DEV
    first_key, second_key = jax.random.split(key, 2)
    cell_keys = jax.random.split(first_key, cells_all)
    orders = jax.vmap(lambda one_key: jax.random.permutation(one_key, position_total))(cell_keys).astype(jnp.int32)
    chosen_cell = jax.random.randint(second_key, (), 0, cells_all)
    corner = position_total - 1
    chosen_order = orders[chosen_cell]
    corner_place = jnp.argmax((chosen_order == corner).astype(jnp.int32))
    swapped = chosen_order.at[corner_place].set(chosen_order[0]).at[0].set(corner)
    orders = orders.at[chosen_cell].set(swapped)
    selected = orders[:, :taken].reshape(cells_all, N_DEPTH, TILES_DEV)
    row_numbers = selected // col_blocks
    col_numbers = selected % col_blocks
    stacked = jnp.stack([row_numbers, col_numbers], 2)
    return stacked.reshape(N_ROW, N_COL, N_DEPTH, 2, TILES_DEV).astype(jnp.int32)


def block_levels(rng, dims, cuts, least, largest):
    factor_of = 1.0
    for axis_at, blocks in cuts:
        heights = jax.random.uniform(jax.random.fold_in(jax.random.fold_in(rng, 6), axis_at), (blocks,), jnp.float32, least / len(cuts), largest / len(cuts))
        factor_of = factor_of * jnp.repeat(jnp.exp(heights), dims[axis_at] // blocks).reshape((-1,) + (1,) * (len(dims) - 1 - axis_at))
    return factor_of


def centred(rng, extent, deviation, most, cuts=(), kind=jnp.bfloat16):
    entries = jax.random.normal(rng, extent, jnp.float32) * deviation
    if len(cuts) > 0:
        entries = block_levels(rng, extent, cuts, -0.22, 0.18) * entries
    return jnp.clip(entries, min=-most, max=most).astype(kind)


def setup_inputs(seed: int = 0) -> dict:
    key_of = jax.random.split(jax.random.key(seed), 7)
    features = centred(key_of[0], (FEAT, NODES), 1.0, 6.0, ((0, 8), (1, 32)))
    weight = centred(key_of[1], (FEAT, FEAT), FEAT ** -0.5, 0.375)
    tiles = centred(key_of[2], (N_ROW, N_COL, N_DEPTH, TILES_DEV, TILE, TILE), (max(TILE, 2 * TILES_DEV * N_DEPTH * TILE * TILE // NODE_DEV)) ** -0.5, 0.03125, ((0, 4), (1, 8), (2, 8)))
    pairs = draw_pairs(jax.random.fold_in(key_of[6], 71), 0)
    counts = draw_counts(jax.random.fold_in(key_of[6], 71), 0)
    cotangent = centred(key_of[5], (FEAT, NODES), 1.0, 6.0, ((0, 8), (1, 32)))
    return dict(features=features, weight=weight, tiles=tiles, pairs=pairs, counts=counts, cotangent=cotangent)


def aggregate(field, tiles, pairs, counts):
    per_piece = NODE_DEV // TILE
    node_blocks = NODES // TILE
    devices_all = N_ROW * N_COL * N_DEPTH
    blocked = field.reshape(FEAT, node_blocks, TILE).transpose(1, 0, 2)
    flat_tiles = tiles.reshape(devices_all, TILES_DEV, TILE, TILE)
    flat_pairs = pairs.reshape(devices_all, 2, TILES_DEV)
    flat_counts = counts.reshape(devices_all)
    slot_index = jnp.arange(TILES_DEV, dtype=jnp.int32)

    def visiting(accumulated, device):
        row_pos = device // (N_COL * N_DEPTH)
        col_pos = (device // N_DEPTH) % N_COL
        local_rows = flat_pairs[device, 0]
        local_cols = flat_pairs[device, 1]
        glob_rows = (row_pos * N_COL * per_piece + local_rows).astype(jnp.int32)
        glob_cols = (((local_cols // per_piece) * N_COL + col_pos) * per_piece + local_cols % per_piece).astype(jnp.int32)
        keep_mask = (slot_index < flat_counts[device]).astype(jnp.float32)
        tile_values = flat_tiles[device].astype(jnp.float32)
        from_cols = blocked[glob_cols].astype(jnp.float32)
        from_rows = blocked[glob_rows].astype(jnp.float32)
        to_rows = jnp.einsum("tfj,tij->tfi", from_cols, tile_values) * keep_mask[:, None, None]
        to_cols = jnp.einsum("tfi,tij->tfj", from_rows, tile_values) * keep_mask[:, None, None]
        accumulated = accumulated.at[glob_rows].add(to_rows).at[glob_cols].add(to_cols)
        return accumulated, None

    initial = jnp.zeros((node_blocks, FEAT, TILE), jnp.float32)
    accumulated, _ = lax.scan(visiting, initial, jnp.arange(devices_all, dtype=jnp.int32))
    return accumulated.transpose(1, 0, 2).reshape(FEAT, NODES)


def reference(features, weight, tiles, pairs, counts, cotangent):
    hidden = jnp.dot(weight.T, features, preferred_element_type=jnp.float32).astype(jnp.bfloat16)
    preact = aggregate(hidden, tiles, pairs, counts)
    activation = jax.nn.silu(preact).astype(jnp.bfloat16)
    sigmoid_pre = jax.nn.sigmoid(preact)
    slope_bf = (cotangent.astype(jnp.float32) * sigmoid_pre * (1.0 + preact * (1.0 - sigmoid_pre))).astype(jnp.bfloat16)
    spread = aggregate(slope_bf, tiles, pairs, counts)
    weight_grad = jnp.dot(features.astype(jnp.float32), spread.T, precision=lax.Precision.HIGHEST)
    return activation, weight_grad
```

```python
import functools

import jax
import jax.numpy as jnp
from jax import lax
from jax.experimental import pallas as pl
from jax.experimental.pallas import tpu as pltpu
from jax.sharding import Mesh, PartitionSpec as P

FEAT = 256
TILE = 128
NODE_DEV = 512
PER_PIECE = NODE_DEV // TILE
HALF = FEAT // 2
GROUP = 4
MIB = 1 << 20

VMEM = pl.BlockSpec(memory_space=pltpu.VMEM)
SMEM = pl.BlockSpec(memory_space=pltpu.SMEM)


def params(mib):
    return pltpu.CompilerParams(vmem_limit_bytes=mib * MIB)


def shifted(value, axes, step):
    total = lax.axis_size(axes)
    return lax.ppermute(value, axes, [(i, (i + step) % total) for i in range(total)])


def order_kernel(place, own, r1, r2, r3, out):
    for back, ref in enumerate((own, r1, r2, r3)):
        slot = lax.rem(place[0] + 4 - back, 4)
        out[pl.ds(pl.multiple_of(slot * 32, 32), 32), :] = ref[...]


def agg_kernel(pieces, outs, transpose, meta, own_tiles, sib_tiles, *refs):
    sources = refs[:pieces]
    results = refs[pieces : pieces + outs]
    field, acc = refs[pieces + outs :]
    for back, ref in enumerate(sources):
        slot = (pieces - back) % pieces
        for part in range(PER_PIECE):
            field[slot * PER_PIECE + part] = ref[:, part * TILE : (part + 1) * TILE]
    acc[...] = jnp.zeros_like(acc)
    contract = (((1,), (1,)), ((), ())) if transpose else (((1,), (0,)), ((), ()))
    for base, tiles in ((0, own_tiles), (3, sib_tiles)):

        def visiting(turn, carry, base=base, tiles=tiles):
            terms = []
            for member in range(GROUP):
                slot = turn * GROUP + member
                terms.append(
                    lax.dot_general(
                        field[meta[base, slot]],
                        tiles[slot],
                        contract,
                        preferred_element_type=jnp.float32,
                    )
                )
            for member in range(GROUP):
                target = meta[base + 1, turn * GROUP + member]
                acc[target] += terms[member]
            return carry

        lax.fori_loop(0, meta[base + 2, 0], visiting, 0)
    for piece in range(outs):
        for part in range(PER_PIECE):
            results[piece][:, part * TILE : (part + 1) * TILE] = acc[
                piece * PER_PIECE + part
            ].astype(jnp.bfloat16)


def agg(meta, own_tiles, sib_tiles, sources, outs, transpose, flops):
    pieces = len(sources)
    piece = jax.ShapeDtypeStruct((HALF, NODE_DEV), jnp.bfloat16)
    return pl.pallas_call(
        functools.partial(agg_kernel, pieces, outs, transpose),
        out_shape=[piece] * outs,
        in_specs=[SMEM, VMEM, VMEM] + [VMEM] * pieces,
        out_specs=[VMEM] * outs,
        scratch_shapes=[
            pltpu.VMEM((pieces * PER_PIECE, HALF, TILE), jnp.bfloat16),
            pltpu.VMEM((outs * PER_PIECE + 1, HALF, TILE), jnp.float32),
        ],
        compiler_params=params(24),
        cost_estimate=pl.CostEstimate(flops=flops, bytes_accessed=6 * MIB, transcendentals=0),
    )(meta, own_tiles, sib_tiles, *sources)


def split(value):
    high = value.astype(jnp.bfloat16)
    low = (value - high.astype(jnp.float32)).astype(jnp.bfloat16)
    return high, low


def dense_kernel(own_ref, sib_ref, weight_own, weight_sib, cotangent, activation, grads):
    own = split(own_ref[...])
    sib = split(sib_ref[...])
    preact = 0.0
    for weight, field in ((weight_own[...], own), (weight_sib[...], sib)):
        for part in field[::-1]:
            preact += jnp.dot(weight, part, preferred_element_type=jnp.float32)
    sigmoid = jax.nn.sigmoid(preact)
    activation[...] = (preact * sigmoid).astype(jnp.bfloat16)
    slope = (
        cotangent[...].astype(jnp.float32) * sigmoid * (1.0 + preact * (1.0 - sigmoid))
    ).astype(jnp.bfloat16)
    for side, field in enumerate((own, sib)):
        total = 0.0
        for part in field[::-1]:
            total += lax.dot_general(
                slope, part, (((1,), (1,)), ((), ())), preferred_element_type=jnp.float32
            )
        for copy in range(grads.shape[0]):
            grads[copy, :, side * HALF : (side + 1) * HALF] = total


def body(features, weight, tiles, pairs, counts, cotangent):
    at_h, at_c = lax.axis_index("h"), lax.axis_index("c")
    at_x = lax.axis_index("x")
    at_yl = lax.axis_index(("y", "l"))
    slot_total = tiles.shape[3]
    own_tiles = tiles.reshape(slot_total, TILE, TILE)
    pair_list = pairs.reshape(2, slot_total)
    count = counts.reshape(())

    keep = jnp.arange(slot_total) < count
    rows = ((pair_list[0] // PER_PIECE - at_yl) % 8) * PER_PIECE + pair_list[0] % PER_PIECE
    cols = ((pair_list[1] // PER_PIECE - at_x) % 4) * PER_PIECE + pair_list[1] % PER_PIECE
    groups = jnp.full((slot_total,), (count + GROUP - 1) // GROUP, jnp.int32)
    own_meta = jnp.stack(
        [
            jnp.where(keep, cols, 0),
            jnp.where(keep, rows, 32),
            jnp.where(keep, rows, 0),
            jnp.where(keep, cols, 16),
            groups,
        ]
    ).astype(jnp.int32)
    sib_meta = shifted(own_meta, "c", 1)
    sib_tiles = shifted(own_tiles, "c", 1)
    both = (own_meta, sib_meta)
    to_rows_meta = jnp.concatenate([m[i : i + 1] for m in both for i in (0, 1, 4)])
    to_cols_meta = jnp.concatenate([m[i : i + 1] for m in both for i in (2, 3, 4)])

    from_h = [shifted(features, "h", k) for k in (1, 2, 3)]
    field = pl.pallas_call(
        order_kernel,
        out_shape=jax.ShapeDtypeStruct((HALF, NODE_DEV), jnp.bfloat16),
        in_specs=[SMEM] + [VMEM] * 4,
        out_specs=VMEM,
    )(at_h.reshape(1), features, *from_h)

    col_seg = [field] + [shifted(field, "x", k) for k in range(1, 4)]
    row_seg = [field] + [shifted(field, ("y", "l"), k) for k in range(1, 8)]
    flops = 2 * 2 * 48 * HALF * TILE * TILE
    row_part = agg(to_rows_meta, own_tiles, sib_tiles, col_seg, 8, True, flops)
    row_got = [shifted(row_part[k], ("y", "l"), k) for k in range(1, 8)]
    col_part = agg(to_cols_meta, own_tiles, sib_tiles, row_seg, 4, False, flops)
    col_got = [shifted(col_part[k], "x", k) for k in range(1, 4)]
    share = sum(
        v.astype(jnp.float32) for v in (row_part[0], col_part[0], *row_got, *col_got)
    ).astype(jnp.bfloat16)
    shares = [share] + [shifted(share, "h", k) for k in (1, 2, 3)]
    total = sum(v.astype(jnp.float32) for v in shares)
    sib_total = shifted(total, "c", 1)

    weight_mine = lax.dynamic_slice_in_dim(weight, (at_h * 2 + at_c) * 32, 32, 1)
    weight_mine = weight_mine.reshape(4, 2, 32, 32)
    weight_own = lax.dynamic_index_in_dim(weight_mine, at_c, 1, False).reshape(HALF, 32).T
    weight_sib = lax.dynamic_index_in_dim(weight_mine, 1 - at_c, 1, False).reshape(HALF, 32).T
    activation, grads = pl.pallas_call(
        dense_kernel,
        out_shape=[
            jax.ShapeDtypeStruct((32, NODE_DEV), jnp.bfloat16),
            jax.ShapeDtypeStruct((32, 32, FEAT), jnp.float32),
        ],
        in_specs=[VMEM] * 5,
        out_specs=[VMEM] * 2,
        compiler_params=params(16),
    )(total, sib_total, weight_own, weight_sib, cotangent)
    grad = lax.all_to_all(grads, ("x", "y", "l"), 0, 0, tiled=True).sum(0)
    own_grad, sib_grad = grad[:, :HALF], grad[:, HALF:]
    first = jnp.where(at_c == 0, own_grad, sib_grad).reshape(32, 4, 32)
    second = jnp.where(at_c == 0, sib_grad, own_grad).reshape(32, 4, 32)
    grad = jnp.stack([first, second], 2).reshape(32, FEAT)
    return activation, grad.T


def solution(mesh):
    fine = Mesh(mesh.devices.reshape(4, 4, 2, 4, 2), ("x", "y", "l", "h", "c"))
    depth, col = ("h", "c"), ("y", "l")
    placed = (
        P(depth, ("x", "y", "l")),
        P(),
        P("x", col, depth, None, None, None),
        P("x", col, depth, None, None),
        P("x", col, depth),
        P(depth, ("x", "y", "l")),
    )
    return jax.shard_map(
        body,
        mesh=fine,
        in_specs=placed,
        out_specs=(P(depth, ("x", "y", "l")), P(None, depth)),
        check_vma=False,
    )
```

```python
import functools

import jax
import jax.numpy as jnp
from jax import lax
from jax.experimental import pallas as pl
from jax.experimental.pallas import tpu as pltpu
from jax.sharding import Mesh, PartitionSpec as P

FEAT = 256
TILE = 128
NODE_DEV = 512
PER_PIECE = NODE_DEV // TILE
HALF = FEAT // 2
GROUP = 32
MIB = 1 << 20
EARLY = 1
PACK = 0
FIN = 0
FLA = 20000000000
FLB = 20000000000

VMEM = pl.BlockSpec(memory_space=pltpu.VMEM)
SMEM = pl.BlockSpec(memory_space=pltpu.SMEM)
ANY = pl.BlockSpec(memory_space=pl.ANY)
HBM = pl.BlockSpec(memory_space=pltpu.HBM)
PIECE = (HALF, NODE_DEV)


def shifted(value, axes, step):
    total = lax.axis_size(axes)
    return lax.ppermute(value, axes, [(i, (i + step) % total) for i in range(total)])


def order_kernel(own, r1, r2, r3, field, arrive):
    place = lax.axis_index("h")
    copies = []
    for back, ref in enumerate((own, r1, r2, r3)):
        slot = lax.rem(place + 4 - back, 4)
        rows = pl.ds(pl.multiple_of(slot * 32, 32), 32)
        copies.append(pltpu.make_async_copy(ref, field.at[rows, :], arrive.at[back]))
    for copy in copies:
        copy.start()
    for copy in copies:
        copy.wait()


def pack_kernel(own, other, both):
    place = lax.axis_index("l")
    both[place] = own[...]
    both[1 - place] = other[...]


def agg_kernel(to_rows, own_meta, sib_meta, own_tiles, sib_tiles, *refs):
    place, place_y = lax.axis_index("x"), lax.axis_index("y")
    if to_rows:
        sources = [refs[-piece % 4] for piece in range(4)]
        result, field, acc, held, staged, tile_sem, field_sem, out_sem = refs[4:]
        outs = 8
    else:
        sources = [refs[-(piece // 2) % 4].at[piece % 2] for piece in range(8)]
        results = refs[4:8]
        field, acc, held, tile_sem, field_sem = refs[8:]
        outs = 4

    sides = ((0, own_meta, own_tiles), (1, sib_meta, sib_tiles))

    def tile_copy(side, turn, tiles):
        return pltpu.make_async_copy(
            tiles.at[pl.ds(turn * GROUP, GROUP)], held.at[side, turn], tile_sem.at[side, turn]
        )

    fills = []
    for piece, source in enumerate(sources):
        for part in range(PER_PIECE):
            lanes = pl.ds(part * TILE, TILE)
            fills.append(
                pltpu.make_async_copy(
                    source.at[:, lanes],
                    field.at[piece * PER_PIECE + part],
                    field_sem.at[piece * PER_PIECE + part],
                )
            )
    for side, meta, tiles in sides:
        tile_copy(side, 0, tiles).start()
    for copy in fills:
        copy.start()
    for side, meta, tiles in sides:

        @pl.when(meta[2, 0] > GROUP)
        def _(side=side, tiles=tiles):
            tile_copy(side, 1, tiles).start()

    acc[...] = jnp.zeros_like(acc)
    for copy in fills:
        copy.wait()
    contract = (((1,), (1,)), ((), ())) if to_rows else (((1,), (0,)), ((), ()))
    for side, meta, tiles in sides:
        used = meta[2, 0]

        def row_of(slot, meta=meta):
            return meta[0, slot]

        def near_row_of(slot, meta=meta):
            return (meta[0, slot] - 2 * PER_PIECE * place_y) & (8 * PER_PIECE - 1)

        def col_of(slot, meta=meta):
            block = meta[1, slot]
            return ((block // PER_PIECE - place) & 3) * PER_PIECE + (block & (PER_PIECE - 1))

        ends = (col_of, row_of) if to_rows else (near_row_of, col_of)

        def visiting(turn, carry, side=side, used=used, tiles=tiles, ends=ends):
            source, target = ends
            tile_copy(side, turn, tiles).wait()
            terms = []
            for member in range(GROUP):
                terms.append(
                    lax.dot_general(
                        field[source(turn * GROUP + member)],
                        held[side, turn, member],
                        contract,
                        preferred_element_type=jnp.float32,
                    )
                )
            for member in range(GROUP):
                slot = turn * GROUP + member
                acc[jnp.where(slot < used, target(slot), outs * PER_PIECE)] += terms[member]
            return carry

        lax.fori_loop(0, (used + GROUP - 1) // GROUP, visiting, 0)
    leaving = []
    for piece in range(outs):
        done = staged.at[piece] if to_rows else results[piece]
        for part in range(PER_PIECE):
            done[:, part * TILE : (part + 1) * TILE] = acc[piece * PER_PIECE + part].astype(
                jnp.bfloat16
            )
        if to_rows:
            leaving.append(pltpu.make_async_copy(done, result.at[piece], out_sem.at[piece]))
            leaving[-1].start()
    for copy in leaving:
        copy.wait()


def agg(to_rows, meta, tiles, sources, flops):
    pieces, outs = (4, 8) if to_rows else (8, 4)
    scratch = [
        pltpu.VMEM((pieces * PER_PIECE, HALF, TILE), jnp.bfloat16),
        pltpu.VMEM((outs * PER_PIECE + 1, HALF, TILE), jnp.float32),
        pltpu.VMEM((2, 64 // GROUP, GROUP, TILE, TILE), jnp.bfloat16),
    ]
    sems = [
        pltpu.SemaphoreType.DMA((2, 64 // GROUP)),
        pltpu.SemaphoreType.DMA((pieces * PER_PIECE,)),
    ]
    if to_rows:
        scratch += [pltpu.VMEM((outs,) + PIECE, jnp.bfloat16)]
        sems += [pltpu.SemaphoreType.DMA((outs,))]
        out_shape, out_specs = jax.ShapeDtypeStruct((outs,) + PIECE, jnp.bfloat16), HBM
    else:
        out_shape, out_specs = [jax.ShapeDtypeStruct(PIECE, jnp.bfloat16)] * outs, [VMEM] * outs
    return pl.pallas_call(
        functools.partial(agg_kernel, to_rows),
        out_shape=out_shape,
        in_specs=[SMEM] * 2 + [HBM] * 2 + [ANY] * len(sources),
        out_specs=out_specs,
        scratch_shapes=scratch + sems,
        compiler_params=pltpu.CompilerParams(vmem_limit_bytes=28 * MIB),
        cost_estimate=pl.CostEstimate(flops=flops, bytes_accessed=6 * MIB, transcendentals=0),
        name="to_rows" if to_rows else "to_cols",
    )(*meta, *tiles, *sources)


def split(value):
    high = value.astype(jnp.bfloat16)
    low = (value - high.astype(jnp.float32)).astype(jnp.bfloat16)
    return high, low


def dense_kernel(own_ref, sib_ref, weight_own, weight_sib, cotangent, activation, grads):
    own = split(own_ref[...])
    sib = split(sib_ref[...])
    preact = 0.0
    for weight, field in ((weight_own[...], own), (weight_sib[...], sib)):
        for part in field[::-1]:
            preact += jnp.dot(weight, part, preferred_element_type=jnp.float32)
    sigmoid = jax.nn.sigmoid(preact)
    activation[...] = (preact * sigmoid).astype(jnp.bfloat16)
    slope = (
        cotangent[...].astype(jnp.float32) * sigmoid * (1.0 + preact * (1.0 - sigmoid))
    ).astype(jnp.bfloat16)
    for side, field in enumerate((own, sib)):
        total = 0.0
        for part in field[::-1]:
            total += lax.dot_general(
                slope, part, (((1,), (1,)), ((), ())), preferred_element_type=jnp.float32
            )
        grads[:, side * HALF : (side + 1) * HALF] = total


def finish_kernel(terms, grad):
    place = lax.axis_index("c")
    total = terms[0].astype(jnp.float32)
    for turn in range(1, terms.shape[0]):
        total += terms[turn].astype(jnp.float32)
    total = total.T
    for side in range(2):
        core = place if side == 0 else 1 - place
        for step in range(4):
            rows = pl.ds(pl.multiple_of(step * 64 + core * 32, 32), 32)
            grad[rows, :] = total[side * HALF + step * 32 : side * HALF + (step + 1) * 32, :]


def body(features, weight, tiles, pairs, counts, cotangent):
    at_h, at_c = lax.axis_index("h"), lax.axis_index("c")
    slot_total = tiles.shape[3]
    own_tiles = tiles.reshape(slot_total, TILE, TILE)
    own_meta = jnp.concatenate(
        [pairs.reshape(2, slot_total), jnp.broadcast_to(counts.reshape(1, 1), (1, slot_total))]
    )
    sib_meta = shifted(own_meta, "c", 1)
    both_tiles = (own_tiles, shifted(own_tiles, "c", 1))

    from_h = [shifted(features, "h", k) for k in (1, 2, 3)]
    if EARLY:
        from_h, sib_meta = lax.optimization_barrier((from_h, sib_meta))
    meta = (own_meta, sib_meta)
    field = pl.pallas_call(
        order_kernel,
        out_shape=jax.ShapeDtypeStruct(PIECE, jnp.bfloat16),
        in_specs=[ANY] * 4,
        out_specs=VMEM,
        scratch_shapes=[pltpu.SemaphoreType.DMA((4,))],
        compiler_params=pltpu.CompilerParams(vmem_limit_bytes=2 * MIB),
        name="order",
    )(features, *from_h)
    other = shifted(field, "l", 1)
    col_seg = [field] + [shifted(field, "x", k) for k in range(1, 4)]
    if PACK == 0:
        near = pl.pallas_call(
            pack_kernel,
            out_shape=jax.ShapeDtypeStruct((2,) + PIECE, jnp.bfloat16),
            in_specs=[VMEM] * 2,
            out_specs=VMEM,
            compiler_params=pltpu.CompilerParams(vmem_limit_bytes=2 * MIB),
            name="pack",
        )(field, other)
    else:
        first = lax.axis_index("l") == 0
        near = jnp.stack([jnp.where(first, field, other), jnp.where(first, other, field)])
    row_seg = [near] + [shifted(near, "y", k) for k in range(1, 4)]
    row_part = agg(True, meta, both_tiles, col_seg, FLA)
    row_got = list(lax.all_to_all(row_part, ("y", "l"), 0, 0, tiled=True))
    col_part = agg(False, meta, both_tiles, row_seg, FLB)
    col_got = [col_part[0]] + [shifted(col_part[k], "x", k) for k in range(1, 4)]
    share = sum(v.astype(jnp.float32) for v in (*row_got, *col_got)).astype(jnp.bfloat16)
    shares = [share] + [shifted(share, "h", k) for k in (1, 2, 3)]
    total = sum(v.astype(jnp.float32) for v in shares)
    sib_total = shifted(total, "c", 1)

    weight_mine = lax.dynamic_slice_in_dim(weight, (at_h * 2 + at_c) * 32, 32, 1)
    weight_mine = weight_mine.reshape(4, 2, 32, 32)
    weight_own = lax.dynamic_index_in_dim(weight_mine, at_c, 1, False).reshape(HALF, 32).T
    weight_sib = lax.dynamic_index_in_dim(weight_mine, 1 - at_c, 1, False).reshape(HALF, 32).T
    activation, grads = pl.pallas_call(
        dense_kernel,
        out_shape=[
            jax.ShapeDtypeStruct((32, NODE_DEV), jnp.bfloat16),
            jax.ShapeDtypeStruct((32, FEAT), jnp.float32),
        ],
        in_specs=[VMEM] * 5,
        out_specs=[VMEM] * 2,
        compiler_params=pltpu.CompilerParams(vmem_limit_bytes=16 * MIB),
        name="dense",
    )(total, sib_total, weight_own, weight_sib, cotangent)
    pair = (grads + shifted(grads, "l", 1)).astype(jnp.bfloat16)
    many = jnp.broadcast_to(pair[None], (16, 32, FEAT))
    terms = lax.all_to_all(many, ("x", "y"), 0, 0, tiled=True)
    grad = pl.pallas_call(
        finish_kernel,
        out_shape=jax.ShapeDtypeStruct((FEAT, 32), jnp.float32),
        in_specs=[VMEM],
        out_specs=VMEM,
        compiler_params=pltpu.CompilerParams(vmem_limit_bytes=2 * MIB),
        name="finish",
    )(terms)
    return activation, grad


def solution(mesh):
    fine = Mesh(mesh.devices.reshape(4, 4, 2, 4, 2), ("x", "y", "l", "h", "c"))
    depth, col = ("h", "c"), ("y", "l")
    placed = (
        P(depth, ("x", "y", "l")),
        P(),
        P("x", col, depth, None, None, None),
        P("x", col, depth, None, None),
        P("x", col, depth),
        P(depth, ("x", "y", "l")),
    )
    return jax.shard_map(
        body,
        mesh=fine,
        in_specs=placed,
        out_specs=(P(depth, ("x", "y", "l")), P(None, depth)),
        check_vma=False,
    )
```

```python
import functools

import jax
import jax.numpy as jnp
from jax import lax
from jax.experimental import pallas as pl
from jax.experimental.pallas import tpu as pltpu
from jax.sharding import Mesh, PartitionSpec as P

FEAT = 256
TILE = 128
NODE_DEV = 512
PER_PIECE = NODE_DEV // TILE
HALF = FEAT // 2
SLOTS = 64
GROUP = 32
MIB = 1 << 20
AGG_FLOPS = 20_000_000_000
AGG_VMEM = 52

VMEM = pl.BlockSpec(memory_space=pltpu.VMEM)
SMEM = pl.BlockSpec(memory_space=pltpu.SMEM)
ANY = pl.BlockSpec(memory_space=pl.ANY)
HBM = pl.BlockSpec(memory_space=pltpu.HBM)
PIECE = (HALF, NODE_DEV)


def limit(mib):
    return pltpu.CompilerParams(vmem_limit_bytes=mib * MIB)


def shifted(value, axis, step):
    total = lax.axis_size(axis)
    return lax.ppermute(value, axis, [(i, (i + step) % total) for i in range(total)])


def ring(values, axis):
    got = [None] * 4
    for step in (2, 1, 3):
        value = values[step] if isinstance(values, (list, tuple)) else values
        got[step] = shifted(value, axis, step)
    return got[1:]


def order_kernel(own, r1, r2, r3, field, arrive):
    place = lax.axis_index("h")
    copies = []
    for back, ref in enumerate((own, r1, r2, r3)):
        slot = lax.rem(place + 4 - back, 4)
        rows = pl.ds(pl.multiple_of(slot * 32, 32), 32)
        copies.append(pltpu.make_async_copy(ref, field.at[rows, :], arrive.at[back]))
    for copy in copies:
        copy.start()
    for copy in copies:
        copy.wait()


def pack_kernel(own, other, both):
    place = lax.axis_index("l")
    both[place] = own[...]
    both[1 - place] = other[...]


def agg_kernel(to_rows, own_meta, sib_meta, own_tiles, sib_tiles, *refs):
    place, place_y = lax.axis_index("x"), lax.axis_index("y")
    if to_rows:
        sources, refs = [refs[-piece % 4] for piece in range(4)], refs[4:]
        result, field, acc, held, staged, tile_sem, out_sem = refs
        outs = 8
    else:
        sources = [refs[-(piece // 2) % 4].at[piece % 2] for piece in range(8)]
        results, (field, acc, held, tile_sem) = refs[4:8], refs[8:]
        outs = 4

    sides = ((0, own_meta, own_tiles), (1, sib_meta, sib_tiles))

    def tile_copy(side, turn, tiles):
        return pltpu.make_async_copy(
            tiles.at[pl.ds(turn * GROUP, GROUP)], held.at[side, turn], tile_sem.at[side, turn]
        )

    for side, meta, tiles in sides:
        for turn in range(SLOTS // GROUP):

            @pl.when(meta[2, 0] > turn * GROUP)
            def _(side=side, turn=turn, tiles=tiles):
                tile_copy(side, turn, tiles).start()

    for piece, source in enumerate(sources):
        for part in range(PER_PIECE):
            field[piece * PER_PIECE + part] = source[:, part * TILE : (part + 1) * TILE]
    acc[...] = jnp.zeros_like(acc)
    contract = (((1,), (1,)), ((), ())) if to_rows else (((1,), (0,)), ((), ()))
    for side, meta, tiles in sides:
        used = meta[2, 0]

        def row_of(slot, meta=meta):
            return meta[0, slot]

        def near_row_of(slot, meta=meta):
            return (meta[0, slot] - 2 * PER_PIECE * place_y) & (8 * PER_PIECE - 1)

        def col_of(slot, meta=meta):
            block = meta[1, slot]
            return ((block // PER_PIECE - place) & 3) * PER_PIECE + (block & (PER_PIECE - 1))

        ends = (col_of, row_of) if to_rows else (near_row_of, col_of)

        def visiting(turn, carry, side=side, used=used, tiles=tiles, ends=ends):
            source, target = ends
            tile_copy(side, turn, tiles).wait()
            terms = []
            for member in range(GROUP):
                terms.append(
                    lax.dot_general(
                        field[source(turn * GROUP + member)],
                        held[side, turn, member],
                        contract,
                        preferred_element_type=jnp.float32,
                    )
                )
            for member in range(GROUP):
                slot = turn * GROUP + member
                acc[jnp.where(slot < used, target(slot), outs * PER_PIECE)] += terms[member]
            return carry

        lax.fori_loop(0, (used + GROUP - 1) // GROUP, visiting, 0)
    leaving = []
    for piece in range(outs):
        done = staged.at[piece] if to_rows else results[piece]
        for part in range(PER_PIECE):
            done[:, part * TILE : (part + 1) * TILE] = acc[piece * PER_PIECE + part].astype(
                jnp.bfloat16
            )
        if to_rows:
            leaving.append(pltpu.make_async_copy(done, result.at[piece], out_sem.at[piece]))
            leaving[-1].start()
    for copy in leaving:
        copy.wait()


def agg(to_rows, meta, tiles, sources):
    pieces, outs = (4, 8) if to_rows else (8, 4)
    scratch = [
        pltpu.VMEM((pieces * PER_PIECE, HALF, TILE), jnp.bfloat16),
        pltpu.VMEM((outs * PER_PIECE + 1, HALF, TILE), jnp.float32),
        pltpu.VMEM((2, SLOTS // GROUP, GROUP, TILE, TILE), jnp.bfloat16),
    ]
    sems = [pltpu.SemaphoreType.DMA((2, SLOTS // GROUP))]
    if to_rows:
        scratch += [pltpu.VMEM((outs,) + PIECE, jnp.bfloat16)]
        sems += [pltpu.SemaphoreType.DMA((outs,))]
        out_shape, out_specs = jax.ShapeDtypeStruct((outs,) + PIECE, jnp.bfloat16), HBM
    else:
        out_shape, out_specs = [jax.ShapeDtypeStruct(PIECE, jnp.bfloat16)] * outs, [VMEM] * outs
    return pl.pallas_call(
        functools.partial(agg_kernel, to_rows),
        out_shape=out_shape,
        in_specs=[SMEM] * 2 + [HBM] * 2 + [VMEM] * len(sources),
        out_specs=out_specs,
        scratch_shapes=scratch + sems,
        compiler_params=limit(AGG_VMEM),
        cost_estimate=pl.CostEstimate(flops=AGG_FLOPS, bytes_accessed=6 * MIB, transcendentals=0),
        name="to_rows" if to_rows else "to_cols",
    )(*meta, *tiles, *sources)


def split(value):
    high = value.astype(jnp.bfloat16)
    low = (value - high.astype(jnp.float32)).astype(jnp.bfloat16)
    return high, low


def dense_kernel(own_ref, sib_ref, weight_own, weight_sib, cotangent, activation, grads):
    own = split(own_ref[...])
    sib = split(sib_ref[...])
    preact = 0.0
    for weight, field in ((weight_own[...], own), (weight_sib[...], sib)):
        for part in field[::-1]:
            preact += jnp.dot(weight, part, preferred_element_type=jnp.float32)
    sigmoid = jax.nn.sigmoid(preact)
    activation[...] = (preact * sigmoid).astype(jnp.bfloat16)
    slope = (
        cotangent[...].astype(jnp.float32) * sigmoid * (1.0 + preact * (1.0 - sigmoid))
    ).astype(jnp.bfloat16)
    for side, field in enumerate((own, sib)):
        total = 0.0
        for part in field[::-1]:
            total += lax.dot_general(
                slope, part, (((1,), (1,)), ((), ())), preferred_element_type=jnp.float32
            )
        grads[:, side * HALF : (side + 1) * HALF] = total


def finish_kernel(terms, grad):
    place = lax.axis_index("c")
    total = terms[0].astype(jnp.float32)
    for turn in range(1, terms.shape[0]):
        total += terms[turn].astype(jnp.float32)
    sides = [
        [total[:, side * HALF + step * 32 : side * HALF + (step + 1) * 32] for step in range(4)]
        for side in range(2)
    ]
    first, second = (
        jnp.concatenate([sides[(side + core) % 2][step] for step in range(4) for side in range(2)], 1)
        for core in range(2)
    )
    grad[...] = jnp.where(place == 0, first, second)


def body(features, weight, tiles, pairs, counts, cotangent):
    at_h, at_c = lax.axis_index("h"), lax.axis_index("c")
    own_tiles = tiles.reshape(SLOTS, TILE, TILE)
    own_meta = jnp.concatenate(
        [pairs.reshape(2, SLOTS), jnp.broadcast_to(counts.reshape(1, 1), (1, SLOTS))]
    )
    sib_meta = shifted(own_meta, "c", 1)
    sib_tiles = shifted(own_tiles, "c", 1)

    from_h = ring(features, "h")
    from_h, sib_meta, sib_tiles = lax.optimization_barrier((from_h, sib_meta, sib_tiles))
    meta, both_tiles = (own_meta, sib_meta), (own_tiles, sib_tiles)
    own_features = jnp.where(counts.reshape(()) >= 0, features, jnp.zeros_like(features))
    field = pl.pallas_call(
        order_kernel,
        out_shape=jax.ShapeDtypeStruct(PIECE, jnp.bfloat16),
        in_specs=[ANY] * 4,
        out_specs=VMEM,
        scratch_shapes=[pltpu.SemaphoreType.DMA((4,))],
        compiler_params=limit(2),
        name="order",
    )(own_features, *from_h)
    other = shifted(field, "l", 1)
    col_seg = [field] + ring(field, "x")
    near = pl.pallas_call(
        pack_kernel,
        out_shape=jax.ShapeDtypeStruct((2,) + PIECE, jnp.bfloat16),
        in_specs=[VMEM] * 2,
        out_specs=VMEM,
        compiler_params=limit(4),
        name="pack",
    )(field, other)
    row_seg = [near] + ring(near, "y")
    row_part = agg(True, meta, both_tiles, col_seg)
    row_got = list(lax.all_to_all(row_part, ("y", "l"), 0, 0, tiled=True))
    col_part = agg(False, meta, both_tiles, row_seg)
    col_got = [col_part[0]] + ring(col_part, "x")
    share = sum(v.astype(jnp.float32) for v in (*row_got, *col_got)).astype(jnp.bfloat16)
    total = sum(v.astype(jnp.float32) for v in [share] + ring(share, "h"))
    sib_total = shifted(total, "c", 1)

    weight_mine = lax.dynamic_slice_in_dim(weight, (at_h * 2 + at_c) * 32, 32, 1)
    weight_mine = weight_mine.reshape(4, 2, 32, 32)
    weight_own = lax.dynamic_index_in_dim(weight_mine, at_c, 1, False).reshape(HALF, 32).T
    weight_sib = lax.dynamic_index_in_dim(weight_mine, 1 - at_c, 1, False).reshape(HALF, 32).T
    activation, grads = pl.pallas_call(
        dense_kernel,
        out_shape=[
            jax.ShapeDtypeStruct((32, NODE_DEV), jnp.bfloat16),
            jax.ShapeDtypeStruct((32, FEAT), jnp.float32),
        ],
        in_specs=[VMEM] * 5,
        out_specs=[VMEM] * 2,
        compiler_params=limit(16),
        name="dense",
    )(total, sib_total, weight_own, weight_sib, cotangent)
    pair = (grads + shifted(grads, "l", 1)).astype(jnp.bfloat16)
    many = jnp.broadcast_to(pair[None], (16, 32, FEAT))
    terms = lax.all_to_all(many, ("x", "y"), 0, 0, tiled=True)
    grad = pl.pallas_call(
        finish_kernel,
        out_shape=jax.ShapeDtypeStruct((32, FEAT), jnp.float32),
        in_specs=[VMEM],
        out_specs=VMEM,
        compiler_params=limit(2),
        name="finish",
    )(terms)
    return activation, grad.T


def solution(mesh):
    fine = Mesh(mesh.devices.reshape(4, 4, 2, 4, 2), ("x", "y", "l", "h", "c"))
    depth, col = ("h", "c"), ("y", "l")
    placed = (
        P(depth, ("x", "y", "l")),
        P(),
        P("x", col, depth, None, None, None),
        P("x", col, depth, None, None),
        P("x", col, depth),
        P(depth, ("x", "y", "l")),
    )
    return jax.shard_map(
        body,
        mesh=fine,
        in_specs=placed,
        out_specs=(P(depth, ("x", "y", "l")), P(None, depth)),
        check_vma=False,
    )
```

```python
import functools

import jax
import jax.numpy as jnp
from jax import lax
from jax.experimental import pallas as pl
from jax.experimental.pallas import tpu as pltpu
from jax.sharding import Mesh, PartitionSpec as P

FEAT = 256
TILE = 128
NODE_DEV = 512
PER_PIECE = NODE_DEV // TILE
HALF = FEAT // 2
SLOTS = 64
GROUP = 32
MIB = 1 << 20
AGG_FLOPS = 20_000_000_000
AGG_VMEM = 52

VMEM = pl.BlockSpec(memory_space=pltpu.VMEM)
SMEM = pl.BlockSpec(memory_space=pltpu.SMEM)
ANY = pl.BlockSpec(memory_space=pl.ANY)
HBM = pl.BlockSpec(memory_space=pltpu.HBM)
PIECE = (HALF, NODE_DEV)


def limit(mib):
    return pltpu.CompilerParams(vmem_limit_bytes=mib * MIB)


def shifted(value, axis, step):
    total = lax.axis_size(axis)
    return lax.ppermute(value, axis, [(i, (i + step) % total) for i in range(total)])


def ring(values, axis):
    got = [None] * 4
    for step in (2, 1, 3):
        value = values[step] if isinstance(values, (list, tuple)) else values
        got[step] = shifted(value, axis, step)
    return got[1:]


def swaps(value, axis):
    return [lax.ppermute(value, axis, [(i, i ^ bits) for i in range(4)]) for bits in (2, 1, 3)]


def order_kernel(own, r1, r2, r3, field, arrive):
    place = lax.axis_index("h")
    copies = []
    for back, ref in enumerate((own, r1, r2, r3)):
        slot = lax.rem(place + 4 - back, 4)
        rows = pl.ds(pl.multiple_of(slot * 32, 32), 32)
        copies.append(pltpu.make_async_copy(ref, field.at[rows, :], arrive.at[back]))
    for copy in copies:
        copy.start()
    for copy in copies:
        copy.wait()


def pack_kernel(own, other, both):
    place = lax.axis_index("l")
    both[place] = own[...]
    both[1 - place] = other[...]


def agg_kernel(to_rows, own_meta, sib_meta, own_tiles, sib_tiles, *refs):
    place, place_y = lax.axis_index("x"), lax.axis_index("y")
    if to_rows:
        sources, refs = [refs[-piece % 4] for piece in range(4)], refs[4:]
        result, field, acc, held, staged, tile_sem, out_sem = refs
        outs = 8
    else:
        sources = [refs[-(piece // 2) % 4].at[piece % 2] for piece in range(8)]
        results, (field, acc, held, tile_sem) = refs[4:8], refs[8:]
        outs = 4

    sides = ((0, own_meta, own_tiles), (1, sib_meta, sib_tiles))

    def tile_copy(side, turn, tiles):
        return pltpu.make_async_copy(
            tiles.at[pl.ds(turn * GROUP, GROUP)], held.at[side, turn], tile_sem.at[side, turn]
        )

    for side, meta, tiles in sides:
        for turn in range(SLOTS // GROUP):

            @pl.when(meta[2, 0] > turn * GROUP)
            def _(side=side, turn=turn, tiles=tiles):
                tile_copy(side, turn, tiles).start()

    for piece, source in enumerate(sources):
        for part in range(PER_PIECE):
            field[piece * PER_PIECE + part] = source[:, part * TILE : (part + 1) * TILE]
    acc[...] = jnp.zeros_like(acc)
    contract = (((1,), (1,)), ((), ())) if to_rows else (((1,), (0,)), ((), ()))
    for side, meta, tiles in sides:
        used = meta[2, 0]

        def row_of(slot, meta=meta):
            return meta[0, slot]

        def near_row_of(slot, meta=meta):
            return (meta[0, slot] - 2 * PER_PIECE * place_y) & (8 * PER_PIECE - 1)

        def col_of(slot, meta=meta):
            block = meta[1, slot]
            return ((block // PER_PIECE - place) & 3) * PER_PIECE + (block & (PER_PIECE - 1))

        ends = (col_of, row_of) if to_rows else (near_row_of, col_of)

        def visiting(turn, carry, side=side, used=used, tiles=tiles, ends=ends):
            source, target = ends
            tile_copy(side, turn, tiles).wait()
            terms = []
            for member in range(GROUP):
                terms.append(
                    lax.dot_general(
                        field[source(turn * GROUP + member)],
                        held[side, turn, member],
                        contract,
                        preferred_element_type=jnp.float32,
                    )
                )
            for member in range(GROUP):
                slot = turn * GROUP + member
                acc[jnp.where(slot < used, target(slot), outs * PER_PIECE)] += terms[member]
            return carry

        lax.fori_loop(0, (used + GROUP - 1) // GROUP, visiting, 0)
    leaving = []
    for piece in range(outs):
        done = staged.at[piece] if to_rows else results[piece]
        for part in range(PER_PIECE):
            done[:, part * TILE : (part + 1) * TILE] = acc[piece * PER_PIECE + part].astype(
                jnp.bfloat16
            )
        if to_rows:
            leaving.append(pltpu.make_async_copy(done, result.at[piece], out_sem.at[piece]))
            leaving[-1].start()
    for copy in leaving:
        copy.wait()


def agg(to_rows, meta, tiles, sources):
    pieces, outs = (4, 8) if to_rows else (8, 4)
    scratch = [
        pltpu.VMEM((pieces * PER_PIECE, HALF, TILE), jnp.bfloat16),
        pltpu.VMEM((outs * PER_PIECE + 1, HALF, TILE), jnp.float32),
        pltpu.VMEM((2, SLOTS // GROUP, GROUP, TILE, TILE), jnp.bfloat16),
    ]
    sems = [pltpu.SemaphoreType.DMA((2, SLOTS // GROUP))]
    if to_rows:
        scratch += [pltpu.VMEM((outs,) + PIECE, jnp.bfloat16)]
        sems += [pltpu.SemaphoreType.DMA((outs,))]
        out_shape, out_specs = jax.ShapeDtypeStruct((outs,) + PIECE, jnp.bfloat16), HBM
    else:
        out_shape, out_specs = [jax.ShapeDtypeStruct(PIECE, jnp.bfloat16)] * outs, [VMEM] * outs
    return pl.pallas_call(
        functools.partial(agg_kernel, to_rows),
        out_shape=out_shape,
        in_specs=[SMEM] * 2 + [HBM] * 2 + [VMEM] * len(sources),
        out_specs=out_specs,
        scratch_shapes=scratch + sems,
        compiler_params=limit(AGG_VMEM),
        cost_estimate=pl.CostEstimate(flops=AGG_FLOPS, bytes_accessed=6 * MIB, transcendentals=0),
        name="to_rows" if to_rows else "to_cols",
    )(*meta, *tiles, *sources)


def split(value):
    high = value.astype(jnp.bfloat16)
    low = (value - high.astype(jnp.float32)).astype(jnp.bfloat16)
    return high, low


def dense_kernel(own_ref, sib_ref, weight_own, weight_sib, cotangent, activation, grads):
    own = split(own_ref[...])
    sib = split(sib_ref[...])
    preact = 0.0
    for weight, field in ((weight_own[...], own), (weight_sib[...], sib)):
        for part in field[::-1]:
            preact += jnp.dot(weight, part, preferred_element_type=jnp.float32)
    sigmoid = jax.nn.sigmoid(preact)
    activation[...] = (preact * sigmoid).astype(jnp.bfloat16)
    slope = (
        cotangent[...].astype(jnp.float32) * sigmoid * (1.0 + preact * (1.0 - sigmoid))
    ).astype(jnp.bfloat16)
    for side, field in enumerate((own, sib)):
        total = 0.0
        for part in field[::-1]:
            total += lax.dot_general(
                slope, part, (((1,), (1,)), ((), ())), preferred_element_type=jnp.float32
            )
        grads[:, side * HALF : (side + 1) * HALF] = total


def finish_kernel(terms, grad):
    place = lax.axis_index("c")
    total = terms[0].astype(jnp.float32)
    for turn in range(1, terms.shape[0]):
        total += terms[turn].astype(jnp.float32)
    sides = [
        [total[:, side * HALF + step * 32 : side * HALF + (step + 1) * 32] for step in range(4)]
        for side in range(2)
    ]
    first, second = (
        jnp.concatenate([sides[(side + core) % 2][step] for step in range(4) for side in range(2)], 1)
        for core in range(2)
    )
    grad[...] = jnp.where(place == 0, first, second)


def body(features, weight, tiles, pairs, counts, cotangent):
    at_h, at_c = lax.axis_index("h"), lax.axis_index("c")
    own_tiles = tiles.reshape(SLOTS, TILE, TILE)
    own_meta = jnp.concatenate(
        [pairs.reshape(2, SLOTS), jnp.broadcast_to(counts.reshape(1, 1), (1, SLOTS))]
    )
    sib_meta = shifted(own_meta, "c", 1)
    sib_tiles = shifted(own_tiles, "c", 1)

    from_h = ring(features, "h")
    from_h, sib_meta, sib_tiles = lax.optimization_barrier((from_h, sib_meta, sib_tiles))
    meta, both_tiles = (own_meta, sib_meta), (own_tiles, sib_tiles)
    own_features = jnp.where(counts.reshape(()) >= 0, features, jnp.zeros_like(features))
    field = pl.pallas_call(
        order_kernel,
        out_shape=jax.ShapeDtypeStruct(PIECE, jnp.bfloat16),
        in_specs=[ANY] * 4,
        out_specs=VMEM,
        scratch_shapes=[pltpu.SemaphoreType.DMA((4,))],
        compiler_params=limit(2),
        name="order",
    )(own_features, *from_h)
    other = shifted(field, "l", 1)
    col_seg = [field] + ring(field, "x")
    near = pl.pallas_call(
        pack_kernel,
        out_shape=jax.ShapeDtypeStruct((2,) + PIECE, jnp.bfloat16),
        in_specs=[VMEM] * 2,
        out_specs=VMEM,
        compiler_params=limit(4),
        name="pack",
    )(field, other)
    row_seg = [near] + ring(near, "y")
    row_part = agg(True, meta, both_tiles, col_seg)
    row_got = list(lax.all_to_all(row_part, ("y", "l"), 0, 0, tiled=True))
    col_part = agg(False, meta, both_tiles, row_seg)
    col_got = [col_part[0]] + ring(col_part, "x")
    share = sum(v.astype(jnp.float32) for v in (*row_got, *col_got)).astype(jnp.bfloat16)
    total = sum(v.astype(jnp.float32) for v in [share] + swaps(share, "h"))
    sib_total = shifted(total, "c", 1)

    weight_mine = lax.dynamic_slice_in_dim(weight, (at_h * 2 + at_c) * 32, 32, 1)
    weight_mine = weight_mine.reshape(4, 2, 32, 32)
    weight_own = lax.dynamic_index_in_dim(weight_mine, at_c, 1, False).reshape(HALF, 32).T
    weight_sib = lax.dynamic_index_in_dim(weight_mine, 1 - at_c, 1, False).reshape(HALF, 32).T
    activation, grads = pl.pallas_call(
        dense_kernel,
        out_shape=[
            jax.ShapeDtypeStruct((32, NODE_DEV), jnp.bfloat16),
            jax.ShapeDtypeStruct((32, FEAT), jnp.float32),
        ],
        in_specs=[VMEM] * 5,
        out_specs=[VMEM] * 2,
        compiler_params=limit(16),
        name="dense",
    )(total, sib_total, weight_own, weight_sib, cotangent)
    pair = (grads + shifted(grads, "l", 1)).astype(jnp.bfloat16)
    many = jnp.broadcast_to(pair[None], (16, 32, FEAT))
    terms = lax.all_to_all(many, ("x", "y"), 0, 0, tiled=True)
    grad = pl.pallas_call(
        finish_kernel,
        out_shape=jax.ShapeDtypeStruct((32, FEAT), jnp.float32),
        in_specs=[VMEM],
        out_specs=VMEM,
        compiler_params=limit(2),
        name="finish",
    )(terms)
    return activation, grad.T


def solution(mesh):
    fine = Mesh(mesh.devices.reshape(4, 4, 2, 4, 2), ("x", "y", "l", "h", "c"))
    depth, col = ("h", "c"), ("y", "l")
    placed = (
        P(depth, ("x", "y", "l")),
        P(),
        P("x", col, depth, None, None, None),
        P("x", col, depth, None, None),
        P("x", col, depth),
        P(depth, ("x", "y", "l")),
    )
    return jax.shard_map(
        body,
        mesh=fine,
        in_specs=placed,
        out_specs=(P(depth, ("x", "y", "l")), P(None, depth)),
        check_vma=False,
    )
```

```python
import functools

import jax
import jax.numpy as jnp
from jax import lax
from jax.experimental import pallas as pl
from jax.experimental.pallas import tpu as pltpu
from jax.sharding import Mesh, PartitionSpec as P

FEAT = 256
TILE = 128
NODE_DEV = 512
PER_PIECE = NODE_DEV // TILE
HALF = FEAT // 2
SLOTS = 64
GROUP = 32
MIB = 1 << 20
AGG_FLOPS = 20_000_000_000
AGG_VMEM = 52

VMEM = pl.BlockSpec(memory_space=pltpu.VMEM)
SMEM = pl.BlockSpec(memory_space=pltpu.SMEM)
ANY = pl.BlockSpec(memory_space=pl.ANY)
HBM = pl.BlockSpec(memory_space=pltpu.HBM)
PIECE = (HALF, NODE_DEV)


def limit(mib):
    return pltpu.CompilerParams(vmem_limit_bytes=mib * MIB)


def shifted(value, axis, step):
    total = lax.axis_size(axis)
    return lax.ppermute(value, axis, [(i, (i + step) % total) for i in range(total)])


def ring(values, axis):
    got = [None] * 4
    for step in (2, 1, 3):
        value = values[step] if isinstance(values, (list, tuple)) else values
        got[step] = shifted(value, axis, step)
    return got[1:]


def swaps(value, axis):
    return [lax.ppermute(value, axis, [(i, i ^ bits) for i in range(4)]) for bits in (2, 1, 3)]


def order_kernel(own, r1, r2, r3, field, arrive):
    place = lax.axis_index("h")
    copies = []
    for back, ref in enumerate((own, r1, r2, r3)):
        slot = lax.rem(place + 4 - back, 4)
        rows = pl.ds(pl.multiple_of(slot * 32, 32), 32)
        copies.append(pltpu.make_async_copy(ref, field.at[rows, :], arrive.at[back]))
    for copy in copies:
        copy.start()
    for copy in copies:
        copy.wait()


def pack_kernel(own, other, both):
    place = lax.axis_index("l")
    both[place] = own[...]
    both[1 - place] = other[...]


def agg_kernel(to_rows, own_meta, sib_meta, own_tiles, sib_tiles, *refs):
    place, place_y = lax.axis_index("x"), lax.axis_index("y")
    if to_rows:
        sources, refs = [refs[-piece % 4] for piece in range(4)], refs[4:]
        result, field, acc, held, staged, tile_sem, out_sem = refs
        outs = 8
    else:
        sources = [refs[-(piece // 2) % 4].at[piece % 2] for piece in range(8)]
        results, (field, acc, held, tile_sem) = refs[4:8], refs[8:]
        outs = 4

    sides = ((0, own_meta, own_tiles), (1, sib_meta, sib_tiles))

    def tile_copy(side, turn, tiles):
        return pltpu.make_async_copy(
            tiles.at[pl.ds(turn * GROUP, GROUP)], held.at[side, turn], tile_sem.at[side, turn]
        )

    for side, meta, tiles in sides:
        for turn in range(SLOTS // GROUP):

            @pl.when(meta[2, 0] > turn * GROUP)
            def _(side=side, turn=turn, tiles=tiles):
                tile_copy(side, turn, tiles).start()

    for piece, source in enumerate(sources):
        for part in range(PER_PIECE):
            field[piece * PER_PIECE + part] = source[:, part * TILE : (part + 1) * TILE]
    acc[...] = jnp.zeros_like(acc)
    contract = (((1,), (1,)), ((), ())) if to_rows else (((1,), (0,)), ((), ()))
    for side, meta, tiles in sides:
        used = meta[2, 0]

        def row_of(slot, meta=meta):
            return meta[0, slot]

        def near_row_of(slot, meta=meta):
            return (meta[0, slot] - 2 * PER_PIECE * place_y) & (8 * PER_PIECE - 1)

        def col_of(slot, meta=meta):
            block = meta[1, slot]
            return ((block // PER_PIECE - place) & 3) * PER_PIECE + (block & (PER_PIECE - 1))

        ends = (col_of, row_of) if to_rows else (near_row_of, col_of)

        def visiting(turn, carry, side=side, used=used, tiles=tiles, ends=ends):
            source, target = ends
            tile_copy(side, turn, tiles).wait()
            terms = []
            for member in range(GROUP):
                terms.append(
                    lax.dot_general(
                        field[source(turn * GROUP + member)],
                        held[side, turn, member],
                        contract,
                        preferred_element_type=jnp.float32,
                    )
                )
            for member in range(GROUP):
                slot = turn * GROUP + member
                acc[jnp.where(slot < used, target(slot), outs * PER_PIECE)] += terms[member]
            return carry

        lax.fori_loop(0, (used + GROUP - 1) // GROUP, visiting, 0)
    leaving = []
    for piece in range(outs):
        done = staged.at[piece] if to_rows else results[piece]
        for part in range(PER_PIECE):
            done[:, part * TILE : (part + 1) * TILE] = acc[piece * PER_PIECE + part].astype(
                jnp.bfloat16
            )
        if to_rows:
            leaving.append(pltpu.make_async_copy(done, result.at[piece], out_sem.at[piece]))
            leaving[-1].start()
    for copy in leaving:
        copy.wait()


def agg(to_rows, meta, tiles, sources):
    pieces, outs = (4, 8) if to_rows else (8, 4)
    scratch = [
        pltpu.VMEM((pieces * PER_PIECE, HALF, TILE), jnp.bfloat16),
        pltpu.VMEM((outs * PER_PIECE + 1, HALF, TILE), jnp.float32),
        pltpu.VMEM((2, SLOTS // GROUP, GROUP, TILE, TILE), jnp.bfloat16),
    ]
    sems = [pltpu.SemaphoreType.DMA((2, SLOTS // GROUP))]
    if to_rows:
        scratch += [pltpu.VMEM((outs,) + PIECE, jnp.bfloat16)]
        sems += [pltpu.SemaphoreType.DMA((outs,))]
        out_shape, out_specs = jax.ShapeDtypeStruct((outs,) + PIECE, jnp.bfloat16), HBM
    else:
        out_shape, out_specs = [jax.ShapeDtypeStruct(PIECE, jnp.bfloat16)] * outs, [VMEM] * outs
    return pl.pallas_call(
        functools.partial(agg_kernel, to_rows),
        out_shape=out_shape,
        in_specs=[SMEM] * 2 + [HBM] * 2 + [VMEM] * len(sources),
        out_specs=out_specs,
        scratch_shapes=scratch + sems,
        compiler_params=limit(AGG_VMEM),
        cost_estimate=pl.CostEstimate(flops=AGG_FLOPS, bytes_accessed=6 * MIB, transcendentals=0),
        name="to_rows" if to_rows else "to_cols",
    )(*meta, *tiles, *sources)


def split(value):
    high = value.astype(jnp.bfloat16)
    low = (value - high.astype(jnp.float32)).astype(jnp.bfloat16)
    return high, low


def dense_kernel(own_ref, sib_ref, weight, cotangent, activation, grads, field):
    place = lax.axis_index("c")
    for core, ref in ((place, own_ref), (1 - place, sib_ref)):
        for step in range(4):
            rows = pl.ds(pl.multiple_of(step * 64 + core * 32, 32), 32)
            field[rows, :] = ref[step * 32 : (step + 1) * 32, :]
    high, low = split(field[...])
    preact = jnp.dot(weight[...], low, preferred_element_type=jnp.float32)
    preact += jnp.dot(weight[...], high, preferred_element_type=jnp.float32)
    sigmoid = jax.nn.sigmoid(preact)
    activation[...] = (preact * sigmoid).astype(jnp.bfloat16)
    slope = (
        cotangent[...].astype(jnp.float32) * sigmoid * (1.0 + preact * (1.0 - sigmoid))
    ).astype(jnp.bfloat16)
    total = 0.0
    for part in (low, high):
        total += lax.dot_general(
            slope, part, (((1,), (1,)), ((), ())), preferred_element_type=jnp.float32
        )
    grads[...] = total


def finish_kernel(terms, grad):
    total = terms[0].astype(jnp.float32)
    for turn in range(1, terms.shape[0]):
        total += terms[turn].astype(jnp.float32)
    grad[...] = total


def body(features, weight, tiles, pairs, counts, cotangent):
    at_h, at_c = lax.axis_index("h"), lax.axis_index("c")
    own_tiles = tiles.reshape(SLOTS, TILE, TILE)
    own_meta = jnp.concatenate(
        [pairs.reshape(2, SLOTS), jnp.broadcast_to(counts.reshape(1, 1), (1, SLOTS))]
    )
    sib_meta = shifted(own_meta, "c", 1)
    sib_tiles = shifted(own_tiles, "c", 1)

    from_h = ring(features, "h")
    from_h, sib_meta, sib_tiles = lax.optimization_barrier((from_h, sib_meta, sib_tiles))
    meta, both_tiles = (own_meta, sib_meta), (own_tiles, sib_tiles)
    own_features = jnp.where(counts.reshape(()) >= 0, features, jnp.zeros_like(features))
    field = pl.pallas_call(
        order_kernel,
        out_shape=jax.ShapeDtypeStruct(PIECE, jnp.bfloat16),
        in_specs=[ANY] * 4,
        out_specs=VMEM,
        scratch_shapes=[pltpu.SemaphoreType.DMA((4,))],
        compiler_params=limit(2),
        name="order",
    )(own_features, *from_h)
    other = shifted(field, "l", 1)
    col_seg = [field] + ring(field, "x")
    near = pl.pallas_call(
        pack_kernel,
        out_shape=jax.ShapeDtypeStruct((2,) + PIECE, jnp.bfloat16),
        in_specs=[VMEM] * 2,
        out_specs=VMEM,
        compiler_params=limit(4),
        name="pack",
    )(field, other)
    row_seg = [near] + ring(near, "y")
    row_part = agg(True, meta, both_tiles, col_seg)
    row_got = list(lax.all_to_all(row_part, ("y", "l"), 0, 0, tiled=True))
    col_part = agg(False, meta, both_tiles, row_seg)
    col_got = [col_part[0]] + ring(col_part, "x")
    share = sum(v.astype(jnp.float32) for v in (*row_got, *col_got)).astype(jnp.bfloat16)
    total = sum(v.astype(jnp.float32) for v in [share] + swaps(share, "h"))
    sib_total = shifted(total, "c", 1)

    weight_mine = lax.dynamic_slice_in_dim(weight, (at_h * 2 + at_c) * 32, 32, 1).T
    activation, grads = pl.pallas_call(
        dense_kernel,
        out_shape=[
            jax.ShapeDtypeStruct((32, NODE_DEV), jnp.bfloat16),
            jax.ShapeDtypeStruct((32, FEAT), jnp.float32),
        ],
        in_specs=[VMEM] * 4,
        out_specs=[VMEM] * 2,
        scratch_shapes=[pltpu.VMEM((FEAT, NODE_DEV), jnp.float32)],
        compiler_params=limit(16),
        name="dense",
    )(total, sib_total, weight_mine, cotangent)
    pair = (grads + shifted(grads, "l", 1)).astype(jnp.bfloat16)
    many = jnp.broadcast_to(pair[None], (16, 32, FEAT))
    terms = lax.all_to_all(many, ("x", "y"), 0, 0, tiled=True)
    grad = pl.pallas_call(
        finish_kernel,
        out_shape=jax.ShapeDtypeStruct((32, FEAT), jnp.float32),
        in_specs=[VMEM],
        out_specs=VMEM,
        compiler_params=limit(2),
        name="finish",
    )(terms)
    return activation, grad.T


def solution(mesh):
    fine = Mesh(mesh.devices.reshape(4, 4, 2, 4, 2), ("x", "y", "l", "h", "c"))
    depth, col = ("h", "c"), ("y", "l")
    placed = (
        P(depth, ("x", "y", "l")),
        P(),
        P("x", col, depth, None, None, None),
        P("x", col, depth, None, None),
        P("x", col, depth),
        P(depth, ("x", "y", "l")),
    )
    return jax.shard_map(
        body,
        mesh=fine,
        in_specs=placed,
        out_specs=(P(depth, ("x", "y", "l")), P(None, depth)),
        check_vma=False,
    )
```

```python
import functools

import jax
import jax.numpy as jnp
from jax import lax
from jax.experimental import pallas as pl
from jax.experimental.pallas import tpu as pltpu
from jax.sharding import Mesh, PartitionSpec as P

FEAT = 256
TILE = 128
NODE_DEV = 512
PER_PIECE = NODE_DEV // TILE
HALF = FEAT // 2
SLOTS = 64
GROUP = 32
MIB = 1 << 20
AGG_FLOPS = 20_000_000_000
AGG_VMEM = 52

VMEM = pl.BlockSpec(memory_space=pltpu.VMEM)
SMEM = pl.BlockSpec(memory_space=pltpu.SMEM)
ANY = pl.BlockSpec(memory_space=pl.ANY)
HBM = pl.BlockSpec(memory_space=pltpu.HBM)
PIECE = (HALF, NODE_DEV)


def limit(mib):
    return pltpu.CompilerParams(vmem_limit_bytes=mib * MIB)


def shifted(value, axis, step):
    total = lax.axis_size(axis)
    return lax.ppermute(value, axis, [(i, (i + step) % total) for i in range(total)])


def ring(values, axis):
    got = [None] * 4
    for step in (2, 1, 3):
        value = values[step] if isinstance(values, (list, tuple)) else values
        got[step] = shifted(value, axis, step)
    return got[1:]


def swaps(value, axis):
    return [lax.ppermute(value, axis, [(i, i ^ bits) for i in range(4)]) for bits in (2, 1, 3)]


def order_kernel(own, r1, r2, r3, field, arrive):
    place = lax.axis_index("h")
    copies = []
    for back, ref in enumerate((own, r1, r2, r3)):
        slot = lax.rem(place + 4 - back, 4)
        rows = pl.ds(pl.multiple_of(slot * 32, 32), 32)
        copies.append(pltpu.make_async_copy(ref, field.at[rows, :], arrive.at[back]))
    for copy in copies:
        copy.start()
    for copy in copies:
        copy.wait()


def pack_kernel(own, other, both):
    place = lax.axis_index("l")
    both[place] = own[...]
    both[1 - place] = other[...]


def agg_kernel(to_rows, own_meta, sib_meta, own_tiles, sib_tiles, *refs):
    place, place_y = lax.axis_index("x"), lax.axis_index("y")
    if to_rows:
        sources, refs = [refs[-piece % 4] for piece in range(4)], refs[4:]
        result, field, acc, held, staged, tile_sem, out_sem = refs
        outs = 8
    else:
        sources = [refs[-(piece // 2) % 4].at[piece % 2] for piece in range(8)]
        results, (field, acc, held, tile_sem) = refs[4:8], refs[8:]
        outs = 4

    sides = ((0, own_meta, own_tiles), (1, sib_meta, sib_tiles))

    def tile_copy(side, turn, tiles):
        return pltpu.make_async_copy(
            tiles.at[pl.ds(turn * GROUP, GROUP)], held.at[side, turn], tile_sem.at[side, turn]
        )

    for side, meta, tiles in sides:
        for turn in range(SLOTS // GROUP):

            @pl.when(meta[2, 0] > turn * GROUP)
            def _(side=side, turn=turn, tiles=tiles):
                tile_copy(side, turn, tiles).start()

    for piece, source in enumerate(sources):
        for part in range(PER_PIECE):
            field[piece * PER_PIECE + part] = source[:, part * TILE : (part + 1) * TILE]
    acc[...] = jnp.zeros_like(acc)
    contract = (((1,), (1,)), ((), ())) if to_rows else (((1,), (0,)), ((), ()))
    for side, meta, tiles in sides:
        used = meta[2, 0]

        def row_of(slot, meta=meta):
            return meta[0, slot]

        def near_row_of(slot, meta=meta):
            return (meta[0, slot] - 2 * PER_PIECE * place_y) & (8 * PER_PIECE - 1)

        def col_of(slot, meta=meta):
            block = meta[1, slot]
            return ((block // PER_PIECE - place) & 3) * PER_PIECE + (block & (PER_PIECE - 1))

        ends = (col_of, row_of) if to_rows else (near_row_of, col_of)

        def visiting(turn, carry, side=side, used=used, tiles=tiles, ends=ends):
            source, target = ends
            tile_copy(side, turn, tiles).wait()
            terms = []
            for member in range(GROUP):
                terms.append(
                    lax.dot_general(
                        field[source(turn * GROUP + member)],
                        held[side, turn, member],
                        contract,
                        preferred_element_type=jnp.float32,
                    )
                )
            for member in range(GROUP):
                slot = turn * GROUP + member
                acc[jnp.where(slot < used, target(slot), outs * PER_PIECE)] += terms[member]
            return carry

        lax.fori_loop(0, (used + GROUP - 1) // GROUP, visiting, 0)
    leaving = []
    for piece in range(outs):
        done = staged.at[piece] if to_rows else results[piece]
        for part in range(PER_PIECE):
            done[:, part * TILE : (part + 1) * TILE] = acc[piece * PER_PIECE + part].astype(
                jnp.bfloat16
            )
        if to_rows:
            leaving.append(pltpu.make_async_copy(done, result.at[piece], out_sem.at[piece]))
            leaving[-1].start()
    for copy in leaving:
        copy.wait()


def agg(to_rows, meta, tiles, sources):
    pieces, outs = (4, 8) if to_rows else (8, 4)
    scratch = [
        pltpu.VMEM((pieces * PER_PIECE, HALF, TILE), jnp.bfloat16),
        pltpu.VMEM((outs * PER_PIECE + 1, HALF, TILE), jnp.float32),
        pltpu.VMEM((2, SLOTS // GROUP, GROUP, TILE, TILE), jnp.bfloat16),
    ]
    sems = [pltpu.SemaphoreType.DMA((2, SLOTS // GROUP))]
    if to_rows:
        scratch += [pltpu.VMEM((outs,) + PIECE, jnp.bfloat16)]
        sems += [pltpu.SemaphoreType.DMA((outs,))]
        out_shape, out_specs = jax.ShapeDtypeStruct((outs,) + PIECE, jnp.bfloat16), HBM
    else:
        out_shape, out_specs = [jax.ShapeDtypeStruct(PIECE, jnp.bfloat16)] * outs, [VMEM] * outs
    return pl.pallas_call(
        functools.partial(agg_kernel, to_rows),
        out_shape=out_shape,
        in_specs=[SMEM] * 2 + [HBM] * 2 + [VMEM] * len(sources),
        out_specs=out_specs,
        scratch_shapes=scratch + sems,
        compiler_params=limit(AGG_VMEM),
        cost_estimate=pl.CostEstimate(flops=AGG_FLOPS, bytes_accessed=6 * MIB, transcendentals=0),
        name="to_rows" if to_rows else "to_cols",
    )(*meta, *tiles, *sources)


def split(value):
    high = value.astype(jnp.bfloat16)
    low = (value - high.astype(jnp.float32)).astype(jnp.bfloat16)
    return high, low


def dense_kernel(own_ref, sib_ref, weight, cotangent, activation, grads, field):
    place = lax.axis_index("c")
    for core, ref in ((place, own_ref), (1 - place, sib_ref)):
        for step in range(4):
            rows = pl.ds(pl.multiple_of(step * 64 + core * 32, 32), 32)
            field[rows, :] = ref[step * 32 : (step + 1) * 32, :].astype(jnp.float32)
    high, low = split(field[...])
    preact = jnp.dot(weight[...], low, preferred_element_type=jnp.float32)
    preact += jnp.dot(weight[...], high, preferred_element_type=jnp.float32)
    sigmoid = jax.nn.sigmoid(preact)
    activation[...] = (preact * sigmoid).astype(jnp.bfloat16)
    slope = (
        cotangent[...].astype(jnp.float32) * sigmoid * (1.0 + preact * (1.0 - sigmoid))
    ).astype(jnp.bfloat16)
    total = 0.0
    for part in (low, high):
        total += lax.dot_general(
            slope, part, (((1,), (1,)), ((), ())), preferred_element_type=jnp.float32
        )
    grads[...] = total


def finish_kernel(terms, grad):
    total = terms[0].astype(jnp.float32)
    for turn in range(1, terms.shape[0]):
        total += terms[turn].astype(jnp.float32)
    grad[...] = total


def body(features, weight, tiles, pairs, counts, cotangent):
    at_h, at_c = lax.axis_index("h"), lax.axis_index("c")
    own_tiles = tiles.reshape(SLOTS, TILE, TILE)
    own_meta = jnp.concatenate(
        [pairs.reshape(2, SLOTS), jnp.broadcast_to(counts.reshape(1, 1), (1, SLOTS))]
    )
    sib_meta = shifted(own_meta, "c", 1)
    sib_tiles = shifted(own_tiles, "c", 1)

    from_h = ring(features, "h")
    from_h, sib_meta, sib_tiles = lax.optimization_barrier((from_h, sib_meta, sib_tiles))
    meta, both_tiles = (own_meta, sib_meta), (own_tiles, sib_tiles)
    own_features = jnp.where(counts.reshape(()) >= 0, features, jnp.zeros_like(features))
    field = pl.pallas_call(
        order_kernel,
        out_shape=jax.ShapeDtypeStruct(PIECE, jnp.bfloat16),
        in_specs=[ANY] * 4,
        out_specs=VMEM,
        scratch_shapes=[pltpu.SemaphoreType.DMA((4,))],
        compiler_params=limit(2),
        name="order",
    )(own_features, *from_h)
    other = shifted(field, "l", 1)
    col_seg = [field] + ring(field, "x")
    near = pl.pallas_call(
        pack_kernel,
        out_shape=jax.ShapeDtypeStruct((2,) + PIECE, jnp.bfloat16),
        in_specs=[VMEM] * 2,
        out_specs=VMEM,
        compiler_params=limit(4),
        name="pack",
    )(field, other)
    row_seg = [near] + ring(near, "y")
    row_part = agg(True, meta, both_tiles, col_seg)
    row_got = list(lax.all_to_all(row_part, ("y", "l"), 0, 0, tiled=True))
    col_part = agg(False, meta, both_tiles, row_seg)
    col_got = [col_part[0]] + ring(col_part, "x")
    share = sum(v.astype(jnp.float32) for v in (*row_got, *col_got)).astype(jnp.bfloat16)
    total = sum(v.astype(jnp.float32) for v in [share] + swaps(share, "h"))
    sib_total = shifted(total.astype(jnp.bfloat16), "c", 1)

    weight_mine = lax.dynamic_slice_in_dim(weight, (at_h * 2 + at_c) * 32, 32, 1).T
    activation, grads = pl.pallas_call(
        dense_kernel,
        out_shape=[
            jax.ShapeDtypeStruct((32, NODE_DEV), jnp.bfloat16),
            jax.ShapeDtypeStruct((32, FEAT), jnp.float32),
        ],
        in_specs=[VMEM] * 4,
        out_specs=[VMEM] * 2,
        scratch_shapes=[pltpu.VMEM((FEAT, NODE_DEV), jnp.float32)],
        compiler_params=limit(16),
        name="dense",
    )(total, sib_total, weight_mine, cotangent)
    pair = (grads + shifted(grads, "l", 1)).astype(jnp.bfloat16)
    many = jnp.broadcast_to(pair[None], (16, 32, FEAT))
    terms = lax.all_to_all(many, ("x", "y"), 0, 0, tiled=True)
    grad = pl.pallas_call(
        finish_kernel,
        out_shape=jax.ShapeDtypeStruct((32, FEAT), jnp.float32),
        in_specs=[VMEM],
        out_specs=VMEM,
        compiler_params=limit(2),
        name="finish",
    )(terms)
    return activation, grad.T


def solution(mesh):
    fine = Mesh(mesh.devices.reshape(4, 4, 2, 4, 2), ("x", "y", "l", "h", "c"))
    depth, col = ("h", "c"), ("y", "l")
    placed = (
        P(depth, ("x", "y", "l")),
        P(),
        P("x", col, depth, None, None, None),
        P("x", col, depth, None, None),
        P("x", col, depth),
        P(depth, ("x", "y", "l")),
    )
    return jax.shard_map(
        body,
        mesh=fine,
        in_specs=placed,
        out_specs=(P(depth, ("x", "y", "l")), P(None, depth)),
        check_vma=False,
    )
```

```python
import functools

import jax
import jax.numpy as jnp
from jax import lax
from jax.experimental import pallas as pl
from jax.experimental.pallas import tpu as pltpu
from jax.sharding import Mesh, PartitionSpec as P

FEAT = 256
TILE = 128
NODE_DEV = 512
PER_PIECE = NODE_DEV // TILE
HALF = FEAT // 2
SLOTS = 64
GROUP = 32
MIB = 1 << 20
AGG_FLOPS = 20_000_000_000
AGG_VMEM = 52

VMEM = pl.BlockSpec(memory_space=pltpu.VMEM)
SMEM = pl.BlockSpec(memory_space=pltpu.SMEM)
ANY = pl.BlockSpec(memory_space=pl.ANY)
HBM = pl.BlockSpec(memory_space=pltpu.HBM)
PIECE = (HALF, NODE_DEV)


def limit(mib):
    return pltpu.CompilerParams(vmem_limit_bytes=mib * MIB)


def shifted(value, axis, step):
    total = lax.axis_size(axis)
    return lax.ppermute(value, axis, [(i, (i + step) % total) for i in range(total)])


def ring(values, axis):
    got = [None] * 4
    for step in (2, 1, 3):
        value = values[step] if isinstance(values, (list, tuple)) else values
        got[step] = shifted(value, axis, step)
    return got[1:]


def swaps(value, axis):
    return [lax.ppermute(value, axis, [(i, i ^ bits) for i in range(4)]) for bits in (2, 1, 3)]


def order_kernel(own, r1, r2, r3, field, arrive):
    place = lax.axis_index("h")
    copies = []
    for back, ref in enumerate((own, r1, r2, r3)):
        slot = lax.rem(place + 4 - back, 4)
        rows = pl.ds(pl.multiple_of(slot * 32, 32), 32)
        copies.append(pltpu.make_async_copy(ref, field.at[rows, :], arrive.at[back]))
    for copy in copies:
        copy.start()
    for copy in copies:
        copy.wait()


def pack_kernel(own, other, both):
    place = lax.axis_index("l")
    both[place] = own[...]
    both[1 - place] = other[...]


def agg_kernel(to_rows, own_meta, sib_meta, own_tiles, sib_tiles, *refs):
    place, place_y = lax.axis_index("x"), lax.axis_index("y")
    if to_rows:
        sources, refs = [refs[-piece % 4] for piece in range(4)], refs[4:]
        result, field, acc, held, staged, tile_sem, out_sem = refs
        outs = 8
    else:
        sources = [refs[-(piece // 2) % 4].at[piece % 2] for piece in range(8)]
        results, (field, acc, held, tile_sem) = refs[4:8], refs[8:]
        outs = 4

    sides = ((0, own_meta, own_tiles), (1, sib_meta, sib_tiles))

    def tile_copy(side, turn, half, tiles):
        return pltpu.make_async_copy(
            tiles.at[pl.ds(turn * GROUP + half * (GROUP // 2), GROUP // 2)],
            held.at[side, turn, pl.ds(half * (GROUP // 2), GROUP // 2)],
            tile_sem.at[side, turn, half],
        )

    for side, meta, tiles in sides:
        for turn in range(SLOTS // GROUP):

            @pl.when(meta[2, 0] > turn * GROUP)
            def _(side=side, turn=turn, tiles=tiles):
                for half in range(2):
                    tile_copy(side, turn, half, tiles).start()

    for piece, source in enumerate(sources):
        for part in range(PER_PIECE):
            field[piece * PER_PIECE + part] = source[:, part * TILE : (part + 1) * TILE]
    acc[...] = jnp.zeros_like(acc)
    contract = (((1,), (1,)), ((), ())) if to_rows else (((1,), (0,)), ((), ()))
    for side, meta, tiles in sides:
        used = meta[2, 0]

        def row_of(slot, meta=meta):
            return meta[0, slot]

        def near_row_of(slot, meta=meta):
            return (meta[0, slot] - 2 * PER_PIECE * place_y) & (8 * PER_PIECE - 1)

        def col_of(slot, meta=meta):
            block = meta[1, slot]
            return ((block // PER_PIECE - place) & 3) * PER_PIECE + (block & (PER_PIECE - 1))

        ends = (col_of, row_of) if to_rows else (near_row_of, col_of)

        def visiting(turn, carry, side=side, used=used, tiles=tiles, ends=ends):
            source, target = ends
            terms = []
            for member in range(GROUP):
                if member % (GROUP // 2) == 0:
                    tile_copy(side, turn, member // (GROUP // 2), tiles).wait()
                terms.append(
                    lax.dot_general(
                        field[source(turn * GROUP + member)],
                        held[side, turn, member],
                        contract,
                        preferred_element_type=jnp.float32,
                    )
                )
            for member in range(GROUP):
                slot = turn * GROUP + member
                acc[jnp.where(slot < used, target(slot), outs * PER_PIECE)] += terms[member]
            return carry

        lax.fori_loop(0, (used + GROUP - 1) // GROUP, visiting, 0)
    leaving = []
    for piece in range(outs):
        done = staged.at[piece] if to_rows else results[piece]
        for part in range(PER_PIECE):
            done[:, part * TILE : (part + 1) * TILE] = acc[piece * PER_PIECE + part].astype(
                jnp.bfloat16
            )
        if to_rows:
            leaving.append(pltpu.make_async_copy(done, result.at[piece], out_sem.at[piece]))
            leaving[-1].start()
    for copy in leaving:
        copy.wait()


def agg(to_rows, meta, tiles, sources):
    pieces, outs = (4, 8) if to_rows else (8, 4)
    scratch = [
        pltpu.VMEM((pieces * PER_PIECE, HALF, TILE), jnp.bfloat16),
        pltpu.VMEM((outs * PER_PIECE + 1, HALF, TILE), jnp.float32),
        pltpu.VMEM((2, SLOTS // GROUP, GROUP, TILE, TILE), jnp.bfloat16),
    ]
    sems = [pltpu.SemaphoreType.DMA((2, SLOTS // GROUP, 2))]
    if to_rows:
        scratch += [pltpu.VMEM((outs,) + PIECE, jnp.bfloat16)]
        sems += [pltpu.SemaphoreType.DMA((outs,))]
        out_shape, out_specs = jax.ShapeDtypeStruct((outs,) + PIECE, jnp.bfloat16), HBM
    else:
        out_shape, out_specs = [jax.ShapeDtypeStruct(PIECE, jnp.bfloat16)] * outs, [VMEM] * outs
    return pl.pallas_call(
        functools.partial(agg_kernel, to_rows),
        out_shape=out_shape,
        in_specs=[SMEM] * 2 + [HBM] * 2 + [VMEM] * len(sources),
        out_specs=out_specs,
        scratch_shapes=scratch + sems,
        compiler_params=limit(AGG_VMEM),
        cost_estimate=pl.CostEstimate(flops=AGG_FLOPS, bytes_accessed=6 * MIB, transcendentals=0),
        name="to_rows" if to_rows else "to_cols",
    )(*meta, *tiles, *sources)


def split(value):
    high = value.astype(jnp.bfloat16)
    low = (value - high.astype(jnp.float32)).astype(jnp.bfloat16)
    return high, low


def dense_kernel(own_ref, sib_ref, weight, cotangent, activation, grads, field):
    place = lax.axis_index("c")
    for core, ref in ((place, own_ref), (1 - place, sib_ref)):
        for step in range(4):
            rows = pl.ds(pl.multiple_of(step * 64 + core * 32, 32), 32)
            field[rows, :] = ref[step * 32 : (step + 1) * 32, :]
    high, low = split(field[...])
    preact = jnp.dot(weight[...], low, preferred_element_type=jnp.float32)
    preact += jnp.dot(weight[...], high, preferred_element_type=jnp.float32)
    sigmoid = jax.nn.sigmoid(preact)
    activation[...] = (preact * sigmoid).astype(jnp.bfloat16)
    slope = (
        cotangent[...].astype(jnp.float32) * sigmoid * (1.0 + preact * (1.0 - sigmoid))
    ).astype(jnp.bfloat16)
    total = 0.0
    for part in (low, high):
        total += lax.dot_general(
            slope, part, (((1,), (1,)), ((), ())), preferred_element_type=jnp.float32
        )
    grads[...] = total


def finish_kernel(terms, grad):
    total = terms[0].astype(jnp.float32)
    for turn in range(1, terms.shape[0]):
        total += terms[turn].astype(jnp.float32)
    grad[...] = total


def body(features, weight, tiles, pairs, counts, cotangent):
    at_h, at_c = lax.axis_index("h"), lax.axis_index("c")
    own_tiles = tiles.reshape(SLOTS, TILE, TILE)
    own_meta = jnp.concatenate(
        [pairs.reshape(2, SLOTS), jnp.broadcast_to(counts.reshape(1, 1), (1, SLOTS))]
    )
    sib_meta = shifted(own_meta, "c", 1)
    sib_tiles = shifted(own_tiles, "c", 1)

    from_h = ring(features, "h")
    from_h, sib_meta, sib_tiles = lax.optimization_barrier((from_h, sib_meta, sib_tiles))
    meta, both_tiles = (own_meta, sib_meta), (own_tiles, sib_tiles)
    own_features = jnp.where(counts.reshape(()) >= 0, features, jnp.zeros_like(features))
    field = pl.pallas_call(
        order_kernel,
        out_shape=jax.ShapeDtypeStruct(PIECE, jnp.bfloat16),
        in_specs=[ANY] * 4,
        out_specs=VMEM,
        scratch_shapes=[pltpu.SemaphoreType.DMA((4,))],
        compiler_params=limit(2),
        name="order",
    )(own_features, *from_h)
    other = shifted(field, "l", 1)
    col_seg = [field] + ring(field, "x")
    near = pl.pallas_call(
        pack_kernel,
        out_shape=jax.ShapeDtypeStruct((2,) + PIECE, jnp.bfloat16),
        in_specs=[VMEM] * 2,
        out_specs=VMEM,
        compiler_params=limit(4),
        name="pack",
    )(field, other)
    row_seg = [near] + ring(near, "y")
    row_part = agg(True, meta, both_tiles, col_seg)
    row_got = list(lax.all_to_all(row_part, ("y", "l"), 0, 0, tiled=True))
    col_part = agg(False, meta, both_tiles, row_seg)
    col_got = [col_part[0]] + ring(col_part, "x")
    share = sum(v.astype(jnp.float32) for v in (*row_got, *col_got)).astype(jnp.bfloat16)
    total = sum(v.astype(jnp.float32) for v in [share] + swaps(share, "h"))
    sib_total = shifted(total, "c", 1)

    weight_mine = lax.dynamic_slice_in_dim(weight, (at_h * 2 + at_c) * 32, 32, 1).T
    activation, grads = pl.pallas_call(
        dense_kernel,
        out_shape=[
            jax.ShapeDtypeStruct((32, NODE_DEV), jnp.bfloat16),
            jax.ShapeDtypeStruct((32, FEAT), jnp.float32),
        ],
        in_specs=[VMEM] * 4,
        out_specs=[VMEM] * 2,
        scratch_shapes=[pltpu.VMEM((FEAT, NODE_DEV), jnp.float32)],
        compiler_params=limit(16),
        name="dense",
    )(total, sib_total, weight_mine, cotangent)
    pair = (grads + shifted(grads, "l", 1)).astype(jnp.bfloat16)
    many = jnp.broadcast_to(pair[None], (16, 32, FEAT))
    terms = lax.all_to_all(many, ("x", "y"), 0, 0, tiled=True)
    grad = pl.pallas_call(
        finish_kernel,
        out_shape=jax.ShapeDtypeStruct((32, FEAT), jnp.float32),
        in_specs=[VMEM],
        out_specs=VMEM,
        compiler_params=limit(2),
        name="finish",
    )(terms)
    return activation, grad.T


def solution(mesh):
    fine = Mesh(mesh.devices.reshape(4, 4, 2, 4, 2), ("x", "y", "l", "h", "c"))
    depth, col = ("h", "c"), ("y", "l")
    placed = (
        P(depth, ("x", "y", "l")),
        P(),
        P("x", col, depth, None, None, None),
        P("x", col, depth, None, None),
        P("x", col, depth),
        P(depth, ("x", "y", "l")),
    )
    return jax.shard_map(
        body,
        mesh=fine,
        in_specs=placed,
        out_specs=(P(depth, ("x", "y", "l")), P(None, depth)),
        check_vma=False,
    )
```
